256 devices in a mesh: chan: 128 (over z, x, y_lo, core), tile: 2 (over y_hi).
Axes of the slice: x: 4, y: 4 (y_hi: 2, y_lo: 2; y = y_hi * 2 + y_lo), z: 8, core: 2. Of those that a mesh axis runs over, the one named last changes fastest.
Arguments:
- voltages: bfloat16 [2, 512, 2, 454656], P(None, 'chan', 'tile'), may hold values from -6 to 6
- filter_taps: float32 [16, 4096], replicated, may hold values from -1.5 to 1.5
- input_good: int32 [512, 2], replicated, may hold values 0 or 1
Outputs:
- visibilities: bfloat16 [256, 8, 512, 512], P('chan', None, 'tile')
The draws below stay inside these ranges and needn't reach their ends.
All inputs are finite; a program needn't handle non-finite values.
Results may differ from the reference program's by a relative error of at most 0.001.
Values sent between devices are 32-bit elements; how exact they have to be, the bound alone decides.
No kernel may reach another device: no remote copies, remote signals or barrier semaphores. Data moves between devices by JAX's collectives and lax.ppermute only.
A program may use at most 128 MiB of HBM per device.

```python
import math
import jax
import jax.numpy as jnp
from jax import lax

STATIONS = 512
NCHAN = 4096
TAPS = 16
SPECTRA = 96
NSAMP = 454656
CORR_CH = 256


def set_ends(array, stream_key, low, top_value):
    spot = [jax.random.randint(jax.random.fold_in(stream_key, axis), (), 0, length) for axis, length in enumerate(array.shape)]
    main_axis = array.shape.index(max(array.shape))
    neighbour = spot[:main_axis] + [(spot[main_axis] + 1) % array.shape[main_axis]] + spot[main_axis + 1:]
    return array.at[tuple(spot)].set(low).at[tuple(neighbour)].set(top_value)


def shard_levels(key, dims, split, least, top_value):
    level, own = 1.0, jax.random.fold_in(key, 6)
    for dim, parts in split:
        steps = jnp.exp(jax.random.uniform(jax.random.fold_in(own, dim), (parts,), jnp.float32, least / len(split), top_value / len(split)))
        level = level * jnp.repeat(steps, dims[dim] // parts).reshape([-1 if axis == dim else 1 for axis in range(len(dims))])
    return level


def noise(stream_key, shape, width, limit, cuts=(), kind=jnp.bfloat16):
    array = jax.random.normal(stream_key, shape, jnp.float32) * width
    if len(cuts) > 0:
        array = shard_levels(stream_key, shape, cuts, -0.22, 0.18) * array
    return jnp.clip(array, min=-limit, max=limit).astype(kind)


def setup_inputs(seed: int = 0) -> dict:
    key_list = jax.random.split(jax.random.key(seed), 4)
    voltages = noise(key_list[0], (2, STATIONS, 2, NSAMP), 1.0, 6.0, ((1, 128), (2, 2)))
    filter_taps = noise(key_list[1], (TAPS, NCHAN), 0.25, 1.5, (), jnp.float32)
    input_good = set_ends((jax.random.randint(key_list[2], (STATIONS, 2), 0, 8) < 7).astype(jnp.int32), jax.random.fold_in(key_list[2], 1), 0, 1)
    return {"voltages": voltages, "filter_taps": filter_taps, "input_good": input_good}


def stokes_planes(corr_real, corr_imag):
    xx_real = corr_real[..., 0, 0, :, :]
    xy_real = corr_real[..., 0, 1, :, :]
    yx_real = corr_real[..., 1, 0, :, :]
    yy_real = corr_real[..., 1, 1, :, :]
    xx_imag = corr_imag[..., 0, 0, :, :]
    xy_imag = corr_imag[..., 0, 1, :, :]
    yx_imag = corr_imag[..., 1, 0, :, :]
    yy_imag = corr_imag[..., 1, 1, :, :]
    planes = (xx_real + yy_real, xx_real - yy_real, xy_real + yx_real, xy_imag - yx_imag, xx_imag + yy_imag, xx_imag - yy_imag, xy_imag + yx_imag, yx_real - xy_real)
    return jnp.stack(planes, axis=-3).astype(jnp.bfloat16)

def channelise(station, filter_taps):
    frames = station.reshape(2, 2, SPECTRA + TAPS - 1, NCHAN)
    filtered = jnp.zeros((2, 2, SPECTRA, NCHAN), jnp.float32)
    for tap_index in range(TAPS):
        filtered = filtered + frames[:, :, tap_index:tap_index + SPECTRA].astype(jnp.float32) * filter_taps[tap_index]
    spectrum = jnp.fft.fft(filtered[0] + 1j * filtered[1], axis=-1)[..., :CORR_CH] / math.sqrt(NCHAN)
    return jnp.stack((jnp.real(spectrum), jnp.imag(spectrum))).astype(jnp.float32)

def reference(voltages, filter_taps, input_good):

    def one_station(index):
        station = lax.dynamic_index_in_dim(voltages, index, 1, keepdims=False)
        return channelise(station, filter_taps)
    spectra = lax.map(one_station, jnp.arange(STATIONS, dtype=jnp.int32))
    mask = input_good.astype(jnp.float32)
    spectra = spectra * mask[:, None, :, None, None]
    per_channel = jnp.transpose(spectra, (4, 1, 2, 0, 3))
    highest = lax.Precision.HIGHEST

    def correlate(channel):
        real_part = channel[0]
        imag_part = channel[1]
        corr_real = (jnp.einsum('pas,qbs->pqab', real_part, real_part, precision=highest) + jnp.einsum('pas,qbs->pqab', imag_part, imag_part, precision=highest)) / SPECTRA
        corr_imag = (jnp.einsum('pas,qbs->pqab', imag_part, real_part, precision=highest) - jnp.einsum('pas,qbs->pqab', real_part, imag_part, precision=highest)) / SPECTRA
        return stokes_planes(corr_real, corr_imag)
    return lax.map(correlate, per_channel)
```

```python
import functools
import math

import jax
import jax.numpy as jnp
import numpy as np
from jax import lax
from jax.experimental import pallas as pl
from jax.experimental.pallas import tpu as pltpu
from jax.sharding import PartitionSpec as P

STATIONS_HERE = 4
CHUNKS = 2
SPECTRA = 96
PART = SPECTRA // CHUNKS
TAPS = 16
FRAMES = SPECTRA + TAPS - 1
NCHAN = 4096
LANES = 128
STEPS = 4
OWNERS = 128
WORD = 2 * PART
ROWS = 2 * STATIONS_HERE * WORD // LANES
VMEM = 56 * 1024 * 1024


@functools.lru_cache(maxsize=None)
def transform_table():
    sample = np.arange(NCHAN // 2).reshape(STEPS, 1, -1, 1)
    channel = 2 * np.arange(OWNERS).reshape(1, 1, 1, -1) + np.arange(2).reshape(1, 2, 1, 1)
    angle = 2.0 * np.pi / NCHAN * (sample * channel % NCHAN)
    table = np.concatenate((np.cos(angle), np.sin(angle)), axis=-1) / math.sqrt(NCHAN)
    high = table.astype(np.float32).astype(jnp.bfloat16)
    low = (table - high.astype(np.float64)).astype(np.float32).astype(jnp.bfloat16)
    return np.stack((high, low), axis=2)


def halves(value):
    high = value.astype(jnp.bfloat16)
    low = (value - high.astype(jnp.float32)).astype(jnp.bfloat16)
    return high, low


def channelise_kernel(first, good_ref, lower_ref, upper_ref, taps_ref, table_ref, out_ref, wide, filtered, total):
    step = pl.program_id(0)
    span = PART + TAPS - 1

    for side, samples in enumerate((lower_ref, upper_ref)):
        tap_ref = taps_ref.at[side]

        def column(index, carry, samples=samples, tap_ref=tap_ref, side=side):
            wide[...] = samples[index, first : first + span].astype(jnp.float32)
            for pair in range(2):
                weights = []
                for tap in range(TAPS):
                    at = 2 * pair * LANES
                    weights.append(
                        jnp.concatenate(
                            (
                                jnp.broadcast_to(tap_ref[tap : tap + 1, at : at + LANES], (4, LANES)),
                                jnp.broadcast_to(tap_ref[tap : tap + 1, at + LANES : at + 2 * LANES], (4, LANES)),
                            ),
                            axis=0,
                        )
                    )
                base = ((side * 2 + index) * 16 + pair * 8) * PART
                sums = {}
                for frame in range(span):
                    sample = wide[frame, 8 * pair : 8 * pair + 8, :]
                    for tap in range(TAPS):
                        spectrum = frame - tap
                        if 0 <= spectrum < PART:
                            term = sample * weights[tap]
                            sums[spectrum] = term if tap == 0 else sums[spectrum] + term
                    done = frame - TAPS + 1
                    if done >= 0:
                        filtered[pl.ds(base + done, 8, stride=PART), :] = sums.pop(done)
            return carry

        lax.fori_loop(0, 2, column, 0)

    rows = STATIONS_HERE * PART

    def block(side, part, line):
        return filtered[pl.ds(((side * 2 + part) * 16 + 4 * line) * PART, rows), :]

    for parity in range(2):
        for part in range(2):
            high, low = [], []
            for line in range(4):
                one, two = block(0, part, line), block(1, part, line)
                h, l = halves(one + two if parity == 0 else one - two)
                high.append(h)
                low.append(l)
            high = jnp.concatenate(high, axis=1)
            low = jnp.concatenate(low, axis=1)
            dot = functools.partial(jnp.dot, preferred_element_type=jnp.float32)
            product = (
                dot(high, table_ref[0, parity, 0])
                + dot(low, table_ref[0, parity, 0])
                + dot(high, table_ref[0, parity, 1])
            )

            @pl.when(step == 0)
            def _(parity=parity, part=part, product=product):
                total[parity, part] = product

            @pl.when(step > 0)
            def _(parity=parity, part=part, product=product):
                total[parity, part] += product

    @pl.when(step == STEPS - 1)
    def _():
        for parity in range(2):
            real = total[parity, 0, :, :LANES] + total[parity, 1, :, LANES:]
            imag = total[parity, 1, :, :LANES] - total[parity, 0, :, LANES:]
            word = []
            for station in range(STATIONS_HERE):
                mask = good_ref[station].astype(jnp.float32)
                at = slice(station * PART, (station + 1) * PART)
                word.append(jnp.concatenate((real[at], imag[at]), axis=0) * mask)
            for row in range(3):
                tile = jnp.concatenate((word[row], word[3][32 * row : 32 * row + 32]), axis=0)
                out_ref[pl.ds(parity * 3 + row, OWNERS, stride=ROWS), :] = tile.T


def channelise(first, good, samples, taps, table):
    return pl.pallas_call(
        functools.partial(channelise_kernel, first),
        grid=(STEPS,),
        in_specs=[
            pl.BlockSpec(memory_space=pltpu.SMEM),
            pl.BlockSpec((2, FRAMES, 16, LANES), lambda q: (0, 0, q, 0)),
            pl.BlockSpec((2, FRAMES, 16, LANES), lambda q: (0, 0, q + STEPS, 0)),
            pl.BlockSpec((2, TAPS, 4 * LANES), lambda q: (0, 0, q)),
            pl.BlockSpec((1, 2, 2, 4 * LANES, 2 * OWNERS), lambda q: (q, 0, 0, 0, 0)),
        ],
        out_specs=pl.BlockSpec((OWNERS * ROWS, LANES), lambda q: (0, 0)),
        out_shape=jax.ShapeDtypeStruct((OWNERS * ROWS, LANES), jnp.float32),
        scratch_shapes=[
            pltpu.VMEM((PART + TAPS - 1, 16, LANES), jnp.float32),
            pltpu.VMEM((2 * 2 * 16 * PART, LANES), jnp.float32),
            pltpu.VMEM((2, 2, STATIONS_HERE * PART, 2 * OWNERS), jnp.float32),
        ],
        compiler_params=pltpu.CompilerParams(vmem_limit_bytes=VMEM),
        cost_estimate=pl.CostEstimate(flops=3_000_000_000, bytes_accessed=12_000_000, transcendentals=0),
        name="channelise",
    )(good, samples, samples, taps, table)


def correlate_kernel(side_ref, own0, own1, other0, other1, out_ref, stations, high, low, turned_high, turned_low):
    parity, section = pl.program_id(0), pl.program_id(1)
    side = side_ref[0]
    lane = lax.broadcasted_iota(jnp.int32, (OWNERS, LANES), 1)

    @pl.when(section == 0)
    def _():
        for which, pair in enumerate(((own0, own1), (other0, other1))):
            slot = side if which == 0 else 1 - side
            for chunk, ref in enumerate(pair):
                rows = [ref[pl.ds(parity * 3 + row, OWNERS, stride=ROWS), :] for row in range(3)]
                for station in range(3):
                    stations[pl.ds(station, OWNERS, stride=4), :] = jnp.where(lane < WORD, rows[station], 0.0)
                last = jnp.where(
                    lane < 32,
                    pltpu.roll(rows[0], 32, 1),
                    jnp.where(lane < 64, pltpu.roll(rows[1], 64, 1), pltpu.roll(rows[2], 96, 1)),
                )
                stations[pl.ds(3, OWNERS, stride=4), :] = jnp.where(lane < WORD, last, 0.0)
                at = slice(chunk * LANES, (chunk + 1) * LANES)
                h, l = halves(stations[...])
                high[slot, :, at] = h
                low[slot, :, at] = l
                mine = stations[pl.ds(pl.multiple_of(side * 256, 256), 256), :]
                column = lax.broadcasted_iota(jnp.int32, (256, LANES), 1)
                turned = jnp.where(
                    column < PART,
                    pltpu.roll(mine, LANES - PART, 1),
                    jnp.where(column < WORD, -pltpu.roll(mine, PART, 1), 0.0),
                )
                h, l = halves(turned)
                turned_high[slot, :, at] = h
                turned_low[slot, :, at] = l

    def product(a_high, a_low, b_high, b_low):
        dot = lambda a, b: lax.dot_general(a, b, (((1,), (1,)), ((), ())), preferred_element_type=jnp.float32)
        return (dot(a_high, b_high) + dot(a_low, b_high) + dot(a_high, b_low)) * (1.0 / SPECTRA)

    first = pl.ds(pl.multiple_of(side * 256 + section * 128, 128), 128)
    local = pl.ds(pl.multiple_of(section * 128, 128), 128)
    real = [[product(high[p, first, :], low[p, first, :], high[q], low[q]) for q in range(2)] for p in range(2)]
    imag = [[product(turned_high[p, local, :], turned_low[p, local, :], high[q], low[q]) for q in range(2)] for p in range(2)]
    planes = (
        real[0][0] + real[1][1],
        real[0][0] - real[1][1],
        real[0][1] + real[1][0],
        imag[0][1] - imag[1][0],
        imag[0][0] + imag[1][1],
        imag[0][0] - imag[1][1],
        imag[0][1] + imag[1][0],
        real[1][0] - real[0][1],
    )
    for index, plane in enumerate(planes):
        out_ref[0, index] = plane.astype(jnp.bfloat16)


def correlate(side, own0, own1, other0, other1):
    whole = pl.BlockSpec((OWNERS * ROWS, LANES), lambda c, a: (0, 0))
    return pl.pallas_call(
        correlate_kernel,
        grid=(2, 2),
        in_specs=[pl.BlockSpec(memory_space=pltpu.SMEM), whole, whole, whole, whole],
        out_specs=pl.BlockSpec((1, 8, 128, 512), lambda c, a: (c, 0, a, 0)),
        out_shape=jax.ShapeDtypeStruct((2, 8, 256, 512), jnp.bfloat16),
        scratch_shapes=[
            pltpu.VMEM((512, LANES), jnp.float32),
            pltpu.VMEM((2, 512, 2 * LANES), jnp.bfloat16),
            pltpu.VMEM((2, 512, 2 * LANES), jnp.bfloat16),
            pltpu.VMEM((2, 256, 2 * LANES), jnp.bfloat16),
            pltpu.VMEM((2, 256, 2 * LANES), jnp.bfloat16),
        ],
        compiler_params=pltpu.CompilerParams(vmem_limit_bytes=VMEM),
        cost_estimate=pl.CostEstimate(flops=3_300_000_000, bytes_accessed=8_000_000, transcendentals=0),
        name="correlate",
    )(side, own0, own1, other0, other1)


def on_device(voltages, filter_taps, input_good):
    table = jnp.asarray(transform_table())
    chan, tile = lax.axis_index("chan"), lax.axis_index("tile")
    samples = voltages.reshape(2, STATIONS_HERE, FRAMES, NCHAN // LANES, LANES)
    samples = samples.transpose(0, 2, 3, 1, 4).reshape(2, FRAMES, LANES, LANES)
    taps = jnp.stack((filter_taps[:, : NCHAN // 2], filter_taps[:, NCHAN // 2 :]))
    good = lax.dynamic_slice(input_good, (chan * STATIONS_HERE, tile), (STATIONS_HERE, 1)).reshape(STATIONS_HERE)
    own, other = [], []
    for chunk in range(CHUNKS):
        spectra = channelise(chunk * PART, good, samples, taps, table)
        spectra = spectra.reshape(OWNERS, 1, ROWS * LANES)
        joined = lax.all_to_all(spectra, "chan", split_axis=0, concat_axis=0, tiled=True)
        joined = joined.reshape(OWNERS * ROWS, LANES)
        own.append(joined)
        other.append(lax.ppermute(joined, "tile", ((0, 1), (1, 0))))
    return correlate(tile.reshape(1).astype(jnp.int32), own[0], own[1], other[0], other[1])


def solution(mesh):
    in_specs = (P(None, "chan", "tile", None), P(), P())
    out_specs = P("chan", None, "tile", None)
    return jax.shard_map(on_device, mesh=mesh, in_specs=in_specs, out_specs=out_specs, check_vma=False)
```

```python
import functools
import math

import jax
import jax.numpy as jnp
import numpy as np
from jax import lax
from jax.experimental import pallas as pl
from jax.experimental.pallas import tpu as pltpu
from jax.sharding import Mesh
from jax.sharding import PartitionSpec as P

STATIONS_HERE = 4
SPECTRA = 96
TAPS = 16
FRAMES = SPECTRA + TAPS - 1
NCHAN = 4096
LANES = 128
STEPS = 4
OWNERS = 128
PARTS = ((0, 64), (64, 32))
AXES = ("z", "x", "yl", "core", "yh")
GROUP = ("z", "x", "core")
PEERS = 64
VMEM = 56 * 1024 * 1024
SMALL_VMEM = 28 * 1024 * 1024


@functools.lru_cache(maxsize=None)
def transform_table():
    sample = np.arange(NCHAN // 2).reshape(STEPS, 1, -1, 1)
    owner = np.arange(OWNERS).reshape(OWNERS // 4, 2, 2).transpose(1, 0, 2)
    channel = 2 * owner.reshape(1, 1, 1, -1) + np.arange(2).reshape(1, 2, 1, 1)
    angle = 2.0 * np.pi / NCHAN * (sample * channel % NCHAN)
    table = np.concatenate((np.cos(angle), np.sin(angle)), axis=-1) / math.sqrt(NCHAN)
    high = table.astype(np.float32).astype(jnp.bfloat16)
    low = (table - high.astype(np.float64)).astype(np.float32).astype(jnp.bfloat16)
    return np.concatenate((high, high, low), axis=2)


def halves(value):
    high = value.astype(jnp.bfloat16)
    low = (value - high.astype(jnp.float32)).astype(jnp.bfloat16)
    return high, low


def channelise_kernel(first, count, good_ref, samples, lower_taps, upper_taps, table_ref, earlier, out_ref, wide, filtered, split, total):
    step = pl.program_id(0)
    rows = STATIONS_HERE * count
    span = count + TAPS - 1
    half = count // 16

    def filter_part(part):
        for side, tap_ref in enumerate((lower_taps, upper_taps)):
            wide[side] = samples[part, first : first + span, side].astype(jnp.float32)
            for pair in range(2):
                weights = []
                for tap in range(TAPS):
                    at = 2 * pair * LANES
                    weights.append(
                        jnp.concatenate(
                            (
                                jnp.broadcast_to(tap_ref[tap : tap + 1, at : at + LANES], (4, LANES)),
                                jnp.broadcast_to(tap_ref[tap : tap + 1, at + LANES : at + 2 * LANES], (4, LANES)),
                            ),
                            axis=0,
                        )
                    )
                base = part * (8 * rows) + (side * 4 + pair * 2) * rows
                sums = {}
                for frame in range(span):
                    sample = wide[side, frame, 8 * pair : 8 * pair + 8, :]
                    for tap in range(TAPS):
                        spectrum = frame - tap
                        if 0 <= spectrum < count:
                            term = sample * weights[tap]
                            sums[spectrum] = term if tap == 0 else sums[spectrum] + term
                    done = frame - TAPS + 1
                    if done >= 0:
                        filtered[pl.ds(base + done, 8, stride=count), :] = sums.pop(done)

    for part in range(2):

        @pl.when(step >= 0)
        def _(part=part):
            filter_part(part)

    for part in range(2):
        for line in range(4):
            start = (part * 8 + line) * rows
            one = filtered[start : start + rows, :]
            two = filtered[start + 4 * rows : start + 5 * rows, :]
            for parity, value in enumerate((one + two, one - two)):
                h, l = halves(value)
                for term, piece in enumerate((h, l, h)):
                    at = (4 * term + line) * LANES
                    split[parity, part * rows : (part + 1) * rows, at : at + LANES] = piece
    for parity in range(2):
        product = jnp.dot(split[parity], table_ref[0, parity], preferred_element_type=jnp.float32)

        @pl.when(step == 0)
        def _(parity=parity, product=product):
            total[parity] = product

        @pl.when(step > 0)
        def _(parity=parity, product=product):
            total[parity] += product

    @pl.when(step == STEPS - 1)
    def _():
        for parity in range(2):
            real = total[parity, :rows, :LANES] + total[parity, rows:, LANES:]
            imag = total[parity, rows:, :LANES] - total[parity, :rows, LANES:]
            words = []
            for station in range(STATIONS_HERE):
                mask = good_ref[station].astype(jnp.float32)
                at = slice(station * count, (station + 1) * count)
                words += [real[at] * mask, imag[at] * mask]
            words = jnp.concatenate(words, axis=0)
            for row in range(half):
                tile = words[row * LANES : (row + 1) * LANES].T
                for low_y in range(2):
                    slot = jnp.where(good_ref[STATIONS_HERE] == low_y, 0, 2 * half)
                    target = pl.ds(slot + parity * half + row, PEERS, stride=4 * half)
                    out_ref[target, :] = tile[low_y * PEERS : (low_y + 1) * PEERS]


def channelise(first, count, good, samples, taps, table, earlier):
    quarter = (1, 2, 12 * LANES, 2 * OWNERS)
    out_rows = PEERS * 4 * (count // 16)
    return pl.pallas_call(
        functools.partial(channelise_kernel, first, count),
        grid=(STEPS,),
        in_specs=[
            pl.BlockSpec(memory_space=pltpu.SMEM),
            pl.BlockSpec((2, FRAMES, 2, 16, LANES), lambda q: (0, 0, 0, q, 0)),
            pl.BlockSpec((TAPS, 4 * LANES), lambda q: (0, q)),
            pl.BlockSpec((TAPS, 4 * LANES), lambda q: (0, q + STEPS)),
            pl.BlockSpec(quarter, lambda q: (q, 0, 0, 0)),
            pl.BlockSpec(memory_space=pl.ANY),
        ],
        out_specs=pl.BlockSpec((out_rows, LANES), lambda q: (0, 0)),
        out_shape=jax.ShapeDtypeStruct((out_rows, LANES), jnp.float32),
        scratch_shapes=[
            pltpu.VMEM((2, count + TAPS - 1, 16, LANES), jnp.float32),
            pltpu.VMEM((2 * 2 * 16 * count, LANES), jnp.float32),
            pltpu.VMEM((2, 2 * STATIONS_HERE * count, 12 * LANES), jnp.bfloat16),
            pltpu.VMEM((2, 2 * STATIONS_HERE * count, 2 * OWNERS), jnp.float32),
        ],
        compiler_params=pltpu.CompilerParams(vmem_limit_bytes=VMEM),
        cost_estimate=pl.CostEstimate(
            flops=125_000_000 * count, bytes_accessed=7_000_000 + 60_000 * count, transcendentals=0
        ),
        name="channelise",
    )(good, samples, taps, taps, table, earlier)


def correlate_kernel(place, *refs):
    pieces, (out_ref, stations, left, right) = (refs[:4], refs[4:8]), refs[8:]
    parity = pl.program_id(0)
    side, low_y = place[0], place[1]
    lane = lax.broadcasted_iota(jnp.int32, (PEERS // 2, LANES), 1)
    column = lax.broadcasted_iota(jnp.int32, (256, LANES), 1)

    for which in range(4):
        slot = 2 * (side if which % 2 == 0 else 1 - side)
        base = 8 * (low_y if which < 2 else 1 - low_y)
        for part, (_, count) in enumerate(PARTS):
            half = count // 16
            buffer = stations.at[slot + part]
            for core in range(2):
                for station in range(STATIONS_HERE):
                    row = parity * half + station * half // STATIONS_HERE
                    word = pieces[part][which][pl.ds(core * 2 * half + row, PEERS // 2, stride=4 * half), :]
                    if part == 1:
                        word = word if station % 2 == 0 else pltpu.roll(word, 64, 1)
                        word = jnp.where(lane < 64, word, 0.0)
                    buffer[pl.ds(base + core * 4 + station, PEERS // 2, stride=16), :] = word

    mine = pl.ds(pl.multiple_of(side * 256, 256), 256)
    for which in range(2):
        for part in range(2):
            at = [slice((2 * term + part) * LANES, (2 * term + part + 1) * LANES) for term in range(3)]
            whole = stations[2 * which + part]
            high, low = halves(whole)
            block = slice(512 * which, 512 * which + 512)
            right[block, at[0]] = high
            right[block, at[1]] = high
            right[block, at[2]] = low
            value = stations[2 * which + part, mine, :]
            if part == 0:
                swapped = pltpu.roll(value, 64, 1)
                turned = jnp.where(column < 64, swapped, -swapped)
            else:
                turned = jnp.where(
                    column < 32, pltpu.roll(value, 96, 1), jnp.where(column < 64, -pltpu.roll(value, 32, 1), 0.0)
                )
            for start, operand in ((256 * which, value), (512 + 256 * which, turned)):
                high, low = halves(operand)
                block = slice(start, start + 256)
                left[block, at[0]] = high
                left[block, at[1]] = low
                left[block, at[2]] = high

    def product(a, b):
        return lax.dot_general(a, b, (((1,), (1,)), ((), ())), preferred_element_type=jnp.float32) * (1.0 / SPECTRA)

    for at in range(0, 512, 256):
        both = [product(left[...], right[512 * q + at : 512 * q + at + 256, :]) for q in range(2)]
        real = [[both[q][256 * p : 256 * p + 256] for q in range(2)] for p in range(2)]
        imag = [[both[q][512 + 256 * p : 768 + 256 * p] for q in range(2)] for p in range(2)]
        planes = (
            real[0][0] + real[1][1],
            real[0][0] - real[1][1],
            real[0][1] + real[1][0],
            imag[0][1] - imag[1][0],
            imag[0][0] + imag[1][1],
            imag[0][0] - imag[1][1],
            imag[0][1] + imag[1][0],
            real[1][0] - real[0][1],
        )
        for index, plane in enumerate(planes):
            out_ref[0, index, :, at : at + 256] = plane.astype(jnp.bfloat16)


def correlate(place, pieces):
    specs = [pl.BlockSpec((PEERS * count // 8, LANES), lambda c: (0, 0)) for _, count in PARTS for _ in range(4)]
    return pl.pallas_call(
        correlate_kernel,
        grid=(2,),
        in_specs=[pl.BlockSpec(memory_space=pltpu.SMEM)] + specs,
        out_specs=pl.BlockSpec((1, 8, 256, 512), lambda c: (c, 0, 0, 0)),
        out_shape=jax.ShapeDtypeStruct((2, 8, 256, 512), jnp.bfloat16),
        scratch_shapes=[
            pltpu.VMEM((4, 512, LANES), jnp.float32),
            pltpu.VMEM((1024, 6 * LANES), jnp.bfloat16),
            pltpu.VMEM((1024, 6 * LANES), jnp.bfloat16),
        ],
        compiler_params=pltpu.CompilerParams(vmem_limit_bytes=SMALL_VMEM),
        cost_estimate=pl.CostEstimate(flops=3_300_000_000, bytes_accessed=8_000_000, transcendentals=0),
        name="correlate",
    )(place, *pieces)


def after(value, token):
    return pl.pallas_call(
        lambda value_ref, token_ref, out_ref: None,
        in_specs=[pl.BlockSpec(memory_space=pl.ANY), pl.BlockSpec(memory_space=pl.ANY)],
        out_specs=pl.BlockSpec(memory_space=pl.ANY),
        out_shape=jax.ShapeDtypeStruct(value.shape, value.dtype),
        input_output_aliases={0: 0},
        name="after",
    )(value, token)


def moves(sizes, target):
    pairs = []
    for z in range(sizes["z"]):
        for x in range(sizes["x"]):
            for y in range(4):
                for core in range(2):
                    source, goal = (
                        (((z * sizes["x"] + x) * 2 + at % 2) * 2 + core) * 2 + at // 2 for at in (y, target(y) % 4)
                    )
                    pairs.append((source, goal))
    return pairs


def on_device(sizes, voltages, filter_taps, input_good):
    table = jnp.asarray(transform_table())
    tile, low_y = lax.axis_index("yh"), lax.axis_index("yl")
    chan = lax.axis_index(("z", "x", "yl", "core"))
    samples = voltages.reshape(2, STATIONS_HERE, FRAMES, NCHAN // LANES, LANES)
    samples = samples.transpose(0, 2, 3, 1, 4).reshape(2, FRAMES, 2, LANES // 2, LANES)
    good = lax.dynamic_slice(input_good, (chan * STATIONS_HERE, tile), (STATIONS_HERE, 1)).reshape(STATIONS_HERE)
    good = jnp.concatenate((good, low_y.reshape(1).astype(jnp.int32)))
    swap = moves(sizes, lambda y: y + 2)
    pair = moves(sizes, lambda y: y ^ 1)
    cross = moves(sizes, lambda y: y - 1 if y % 2 == 0 else y + 1)
    pieces, earlier, token = [], filter_taps, None
    for first, count in PARTS:
        width = count // 8 * LANES
        earlier = channelise(first, count, good, samples, filter_taps, table, earlier)
        spectra = earlier if token is None else after(earlier, token)
        spectra = spectra.reshape(PEERS, 1, 2 * width)
        joined = lax.all_to_all(spectra, GROUP, split_axis=0, concat_axis=0, tiled=True)
        token = joined[0, :, :LANES]
        near, far = (joined[:, :, at : at + width].reshape(-1, LANES) for at in (0, width))
        pieces += [near] + [lax.ppermute(block, AXES, pairs) for block, pairs in ((near, swap), (far, pair), (far, cross))]
    place = jnp.stack((tile, low_y)).astype(jnp.int32)
    return correlate(place, pieces)


def solution(mesh):
    sizes = {"z": 8, "x": 4, "yl": 2, "core": 2, "yh": 2}
    fine = Mesh(mesh.devices.reshape(tuple(sizes[axis] for axis in AXES)), AXES)
    in_specs = (P(None, ("z", "x", "yl", "core"), "yh", None), P(), P())
    out_specs = P(("z", "x", "yl", "core"), None, "yh", None)
    return jax.shard_map(
        functools.partial(on_device, sizes), mesh=fine, in_specs=in_specs, out_specs=out_specs, check_vma=False
    )
```

```python
import functools
import math

import jax
import jax.numpy as jnp
import numpy as np
from jax import lax
from jax.experimental import pallas as pl
from jax.experimental.pallas import tpu as pltpu
from jax.sharding import Mesh
from jax.sharding import PartitionSpec as P

STATIONS_HERE = 4
SPECTRA = 96
TAPS = 16
FRAMES = SPECTRA + TAPS - 1
NCHAN = 4096
LANES = 128
STEPS = 4
OWNERS = 128
PARTS = ((0, 64), (64, 32))
SHORT = 4
AXES = ("z", "x", "yl", "core", "yh")
GROUP = ("z", "x", "core")
PEERS = 64
VMEM = 56 * 1024 * 1024
SMALL_VMEM = 28 * 1024 * 1024


@functools.lru_cache(maxsize=None)
def transform_table():
    sample = np.arange(NCHAN // 2).reshape(STEPS, 1, -1, 1)
    owner = np.arange(OWNERS).reshape(OWNERS // 4, 2, 2).transpose(1, 0, 2)
    channel = 2 * owner.reshape(1, 1, 1, -1) + np.arange(2).reshape(1, 2, 1, 1)
    angle = 2.0 * np.pi / NCHAN * (sample * channel % NCHAN)
    table = np.concatenate((np.cos(angle), np.sin(angle)), axis=-1) / math.sqrt(NCHAN)
    high = table.astype(np.float32).astype(jnp.bfloat16)
    low = (table - high.astype(np.float64)).astype(np.float32).astype(jnp.bfloat16)
    return np.concatenate((high, high, low), axis=2)


def halves(value):
    high = value.astype(jnp.bfloat16)
    low = (value - high.astype(jnp.float32)).astype(jnp.bfloat16)
    return high, low


def fir(lines, weights, count):
    taps = len(weights)
    if taps <= SHORT:
        out = []
        for j in range(count):
            value = weights[0] * lines[j]
            for m in range(1, taps):
                value = value + weights[m] * lines[j + m]
            out.append(value)
        return out
    pairs = count // 2
    even, odd = lines[0::2], lines[1::2]
    both = [odd[t] + even[t + 1] for t in range(min(len(odd), len(even) - 1))]
    a = fir(even, weights[0::2], pairs + 1)
    b = fir(odd, weights[1::2], pairs)
    c = fir(both, [u + v for u, v in zip(weights[0::2], weights[1::2])], pairs)
    out = []
    for t in range(pairs):
        out += [a[t] + b[t], c[t] - a[t + 1] - b[t]]
    if count % 2:
        out.append(a[pairs] + fir(odd[pairs:], weights[1::2], 1)[0])
    return out


def channelise_kernel(count, good_ref, chan_ref, tile_ref, low_y_ref, samples, lower_taps, upper_taps, table_ref, earlier, out_ref, wide, filtered, split, total):
    step = pl.program_id(0)
    rows = STATIONS_HERE * count
    span = count + TAPS - 1
    half = count // 16

    def filter_part(part):
        for side, tap_ref in enumerate((lower_taps, upper_taps)):
            wide[side] = samples[part, :, side].astype(jnp.float32)
            for pair in range(2):
                weights = []
                for tap in range(TAPS):
                    at = 2 * pair * LANES
                    weights.append(
                        jnp.concatenate(
                            (
                                jnp.broadcast_to(tap_ref[tap : tap + 1, at : at + LANES], (4, LANES)),
                                jnp.broadcast_to(tap_ref[tap : tap + 1, at + LANES : at + 2 * LANES], (4, LANES)),
                            ),
                            axis=0,
                        )
                    )
                base = part * (8 * rows) + (side * 4 + pair * 2) * rows
                lines = [wide[side, frame, 8 * pair : 8 * pair + 8, :] for frame in range(span)]
                for spectrum, value in enumerate(fir(lines, weights, count)):
                    filtered[pl.ds(base + spectrum, 8, stride=count), :] = value

    for part in range(2):

        @pl.when(step >= 0)
        def _(part=part):
            filter_part(part)

    for part in range(2):
        for line in range(4):
            start = (part * 8 + line) * rows
            one = filtered[start : start + rows, :]
            two = filtered[start + 4 * rows : start + 5 * rows, :]
            for parity, value in enumerate((one + two, one - two)):
                h, l = halves(value)
                for term, piece in enumerate((h, l, h)):
                    at = (4 * term + line) * LANES
                    split[parity, part * rows : (part + 1) * rows, at : at + LANES] = piece
    for parity in range(2):
        product = jnp.dot(split[parity], table_ref[0, parity], preferred_element_type=jnp.float32)

        @pl.when(step == 0)
        def _(parity=parity, product=product):
            total[parity] = product

        @pl.when(step > 0)
        def _(parity=parity, product=product):
            total[parity] += product

    @pl.when(step == STEPS - 1)
    def _():
        for parity in range(2):
            real = total[parity, :rows, :LANES] + total[parity, rows:, LANES:]
            imag = total[parity, rows:, :LANES] - total[parity, :rows, LANES:]
            words = []
            for station in range(STATIONS_HERE):
                mask = good_ref[tile_ref[0], chan_ref[0] * STATIONS_HERE + station].astype(jnp.float32)
                at = slice(station * count, (station + 1) * count)
                words += [real[at] * mask, imag[at] * mask]
            words = jnp.concatenate(words, axis=0)
            for row in range(half):
                tile = words[row * LANES : (row + 1) * LANES].T
                for low_y in range(2):
                    slot = jnp.where(low_y_ref[0] == low_y, 0, 2 * half)
                    target = pl.ds(slot + parity * half + row, PEERS, stride=4 * half)
                    out_ref[target, :] = tile[low_y * PEERS : (low_y + 1) * PEERS]


def channelise(first, count, place, good, samples, taps, table, earlier):
    quarter = (1, 2, 12 * LANES, 2 * OWNERS)
    out_rows = PEERS * 4 * (count // 16)
    return pl.pallas_call(
        functools.partial(channelise_kernel, count),
        grid=(STEPS,),
        in_specs=[
            pl.BlockSpec(memory_space=pltpu.SMEM),
            pl.BlockSpec(memory_space=pltpu.SMEM),
            pl.BlockSpec(memory_space=pltpu.SMEM),
            pl.BlockSpec(memory_space=pltpu.SMEM),
            pl.BlockSpec(
                (pl.Element(2), pl.Element(count + TAPS - 1), pl.Element(2), pl.Element(16), pl.Element(LANES)),
                lambda q: (0, first, 0, 16 * q, 0),
            ),
            pl.BlockSpec((TAPS, 4 * LANES), lambda q: (0, q)),
            pl.BlockSpec((TAPS, 4 * LANES), lambda q: (0, q + STEPS)),
            pl.BlockSpec(quarter, lambda q: (q, 0, 0, 0)),
            pl.BlockSpec(memory_space=pl.ANY),
        ],
        out_specs=pl.BlockSpec((out_rows, LANES), lambda q: (0, 0)),
        out_shape=jax.ShapeDtypeStruct((out_rows, LANES), jnp.float32),
        scratch_shapes=[
            pltpu.VMEM((2, count + TAPS - 1, 16, LANES), jnp.float32),
            pltpu.VMEM((2 * 2 * 16 * count, LANES), jnp.float32),
            pltpu.VMEM((2, 2 * STATIONS_HERE * count, 12 * LANES), jnp.bfloat16),
            pltpu.VMEM((2, 2 * STATIONS_HERE * count, 2 * OWNERS), jnp.float32),
        ],
        compiler_params=pltpu.CompilerParams(vmem_limit_bytes=VMEM),
        cost_estimate=pl.CostEstimate(
            flops=125_000_000 * count, bytes_accessed=7_000_000 + 60_000 * count, transcendentals=0
        ),
        name="channelise",
    )(good, *place, samples, taps, taps, table, earlier)


def correlate_kernel(tile_ref, low_y_ref, *refs):
    pieces, (out_ref, stations, left, right) = (refs[:4], refs[4:8]), refs[8:]
    parity = pl.program_id(0)
    side, low_y = tile_ref[0], low_y_ref[0]
    lane = lax.broadcasted_iota(jnp.int32, (PEERS // 2, LANES), 1)
    column = lax.broadcasted_iota(jnp.int32, (256, LANES), 1)

    for which in range(4):
        slot = 2 * (side if which % 2 == 0 else 1 - side)
        base = 8 * (low_y if which < 2 else 1 - low_y)
        for part, (_, count) in enumerate(PARTS):
            half = count // 16
            buffer = stations.at[slot + part]
            for core in range(2):
                for station in range(STATIONS_HERE):
                    row = parity * half + station * half // STATIONS_HERE
                    word = pieces[part][which][pl.ds(core * 2 * half + row, PEERS // 2, stride=4 * half), :]
                    if part == 1:
                        word = word if station % 2 == 0 else pltpu.roll(word, 64, 1)
                        word = jnp.where(lane < 64, word, 0.0)
                    buffer[pl.ds(base + core * 4 + station, PEERS // 2, stride=16), :] = word

    mine = pl.ds(pl.multiple_of(side * 256, 256), 256)
    for which in range(2):
        for part in range(2):
            at = [slice((2 * term + part) * LANES, (2 * term + part + 1) * LANES) for term in range(3)]
            whole = stations[2 * which + part]
            high, low = halves(whole)
            block = slice(512 * which, 512 * which + 512)
            right[block, at[0]] = high
            right[block, at[1]] = high
            right[block, at[2]] = low
            value = stations[2 * which + part, mine, :]
            if part == 0:
                swapped = pltpu.roll(value, 64, 1)
                turned = jnp.where(column < 64, swapped, -swapped)
            else:
                turned = jnp.where(
                    column < 32, pltpu.roll(value, 96, 1), jnp.where(column < 64, -pltpu.roll(value, 32, 1), 0.0)
                )
            for start, operand in ((256 * which, value), (512 + 256 * which, turned)):
                high, low = halves(operand * (1.0 / SPECTRA))
                block = slice(start, start + 256)
                left[block, at[0]] = high
                left[block, at[1]] = low
                left[block, at[2]] = high

    def product(a, b):
        return lax.dot_general(a, b, (((1,), (1,)), ((), ())), preferred_element_type=jnp.float32)

    for at in range(0, 512, 256):
        both = [product(left[...], right[512 * q + at : 512 * q + at + 256, :]) for q in range(2)]
        real = [[both[q][256 * p : 256 * p + 256] for q in range(2)] for p in range(2)]
        imag = [[both[q][512 + 256 * p : 768 + 256 * p] for q in range(2)] for p in range(2)]
        planes = (
            real[0][0] + real[1][1],
            real[0][0] - real[1][1],
            real[0][1] + real[1][0],
            imag[0][1] - imag[1][0],
            imag[0][0] + imag[1][1],
            imag[0][0] - imag[1][1],
            imag[0][1] + imag[1][0],
            real[1][0] - real[0][1],
        )
        for index, plane in enumerate(planes):
            out_ref[0, index, :, at : at + 256] = plane.astype(jnp.bfloat16)


def correlate(tile, low_y, pieces):
    specs = [pl.BlockSpec((PEERS * count // 8, LANES), lambda c: (0, 0)) for _, count in PARTS for _ in range(4)]
    return pl.pallas_call(
        correlate_kernel,
        grid=(2,),
        in_specs=[pl.BlockSpec(memory_space=pltpu.SMEM)] * 2 + specs,
        out_specs=pl.BlockSpec((1, 8, 256, 512), lambda c: (c, 0, 0, 0)),
        out_shape=jax.ShapeDtypeStruct((2, 8, 256, 512), jnp.bfloat16),
        scratch_shapes=[
            pltpu.VMEM((4, 512, LANES), jnp.float32),
            pltpu.VMEM((1024, 6 * LANES), jnp.bfloat16),
            pltpu.VMEM((1024, 6 * LANES), jnp.bfloat16),
        ],
        compiler_params=pltpu.CompilerParams(vmem_limit_bytes=SMALL_VMEM),
        cost_estimate=pl.CostEstimate(flops=3_300_000_000, bytes_accessed=8_000_000, transcendentals=0),
        name="correlate",
    )(tile, low_y, *pieces)


def after(value, token):
    return pl.pallas_call(
        lambda value_ref, token_ref, out_ref: None,
        in_specs=[pl.BlockSpec(memory_space=pl.ANY), pl.BlockSpec(memory_space=pl.ANY)],
        out_specs=pl.BlockSpec(memory_space=pl.ANY),
        out_shape=jax.ShapeDtypeStruct(value.shape, value.dtype),
        input_output_aliases={0: 0},
        name="after",
    )(value, token)


def moves(sizes, target):
    pairs = []
    for z in range(sizes["z"]):
        for x in range(sizes["x"]):
            for y in range(4):
                for core in range(2):
                    source, goal = (
                        (((z * sizes["x"] + x) * 2 + at % 2) * 2 + core) * 2 + at // 2 for at in (y, target(y) % 4)
                    )
                    pairs.append((source, goal))
    return pairs


def on_device(sizes, voltages, filter_taps, input_good):
    table = jnp.asarray(transform_table())
    tile, low_y = lax.axis_index("yh"), lax.axis_index("yl")
    chan = lax.axis_index(("z", "x", "yl", "core"))
    samples = voltages.reshape(2, STATIONS_HERE, FRAMES, NCHAN // LANES, LANES)
    samples = samples.transpose(0, 2, 3, 1, 4).reshape(2, FRAMES, 2, LANES // 2, LANES)
    chan, tile, low_y = (index.reshape(1).astype(jnp.int32) for index in (chan, tile, low_y))
    swap = moves(sizes, lambda y: y + 2)
    pair = moves(sizes, lambda y: y ^ 1)
    cross = moves(sizes, lambda y: y - 1 if y % 2 == 0 else y + 1)
    pieces, earlier, token = [], filter_taps, None
    for first, count in PARTS:
        width = count // 8
        earlier = channelise(first, count, (chan, tile, low_y), input_good.T, samples, filter_taps, table, earlier)
        spectra = earlier if token is None else after(earlier, token)
        spectra = spectra.reshape(PEERS, 2 * width, LANES)
        joined = lax.all_to_all(spectra, GROUP, split_axis=0, concat_axis=0, tiled=True)
        token = joined[0, :8]
        near, far = (joined[:, at : at + width].reshape(-1, LANES) for at in (0, width))
        pieces += [near] + [lax.ppermute(block, AXES, pairs) for block, pairs in ((near, swap), (far, pair), (far, cross))]
    return correlate(tile, low_y, pieces)


def solution(mesh):
    sizes = {"z": 8, "x": 4, "yl": 2, "core": 2, "yh": 2}
    fine = Mesh(mesh.devices.reshape(tuple(sizes[axis] for axis in AXES)), AXES)
    in_specs = (P(None, ("z", "x", "yl", "core"), "yh", None), P(), P())
    out_specs = P(("z", "x", "yl", "core"), None, "yh", None)
    return jax.shard_map(
        functools.partial(on_device, sizes), mesh=fine, in_specs=in_specs, out_specs=out_specs, check_vma=False
    )
```

```python
import functools
import math

import jax
import jax.numpy as jnp
import numpy as np
from jax import lax
from jax.experimental import pallas as pl
from jax.experimental.pallas import tpu as pltpu
from jax.sharding import Mesh
from jax.sharding import PartitionSpec as P

STATIONS_HERE = 4
SPECTRA = 96
TAPS = 16
FRAMES = SPECTRA + TAPS - 1
NCHAN = 4096
LANES = 128
STEPS = 2
RADIX = 4
OWNERS = 128
PARTS = ((0, 64), (64, 32))
SHORT = 8
BLOCK = 16
CUT = 64
AXES = ("z", "x", "yl", "core", "yh")
GROUP = ("z", "x", "core")
PEERS = 64
VMEM = 56 * 1024 * 1024
SMALL_VMEM = 28 * 1024 * 1024


@functools.lru_cache(maxsize=None)
def transform_table():
    sample = np.arange(NCHAN // RADIX).reshape(STEPS, 1, -1, 1)
    order = np.arange(OWNERS // 2).reshape(OWNERS // 4, 2).T.reshape(1, 1, 1, -1)
    rest = np.arange(RADIX).reshape(1, RADIX, 1, 1)
    angle = 2.0 * np.pi / NCHAN * (sample * (RADIX * order + rest) % NCHAN)
    cosine, sine = np.cos(angle) / math.sqrt(NCHAN), np.sin(angle) / math.sqrt(NCHAN)
    real = np.concatenate((cosine, sine), axis=2)
    imag = np.concatenate((-sine, cosine), axis=2)
    table = np.where(rest < 2, np.concatenate((real, imag), axis=3), np.concatenate((imag, real), axis=3))
    high = table.astype(np.float32).astype(jnp.bfloat16)
    low = (table - high.astype(np.float64)).astype(np.float32).astype(jnp.bfloat16)
    return np.concatenate((high, low), axis=3)


def halves(value):
    high = value.astype(jnp.bfloat16)
    low = (value - high.astype(jnp.float32)).astype(jnp.bfloat16)
    return high, low


def fir(lines, weights, count):
    taps = len(weights)
    if taps <= SHORT:
        out = []
        for j in range(count):
            value = weights[0] * lines[j]
            for m in range(1, taps):
                value = value + weights[m] * lines[j + m]
            out.append(value)
        return out
    pairs = count // 2
    even, odd = lines[0::2], lines[1::2]
    both = [odd[t] + even[t + 1] for t in range(min(len(odd), len(even) - 1))]
    a = fir(even, weights[0::2], pairs + 1)
    b = fir(odd, weights[1::2], pairs)
    c = fir(both, [u + v for u, v in zip(weights[0::2], weights[1::2])], pairs)
    out = []
    for t in range(pairs):
        out += [a[t] + b[t], c[t] - a[t + 1] - b[t]]
    if count % 2:
        out.append(a[pairs] + fir(odd[pairs:], weights[1::2], 1)[0])
    return out


def channelise_kernel(count, good_ref, chan_ref, tile_ref, low_y_ref, samples, *refs):
    taps_ref, table_ref, _, out_ref, wide, filtered, split, total, table, arrived = refs
    step = pl.program_id(0)
    rows = STATIONS_HERE * count
    span = count + TAPS - 1
    half = count // 16

    def filter_lines(index, carry):
        part, quarter = index // RADIX, index % RADIX
        wide[...] = samples[part, :, quarter].astype(jnp.float32)
        for pair in range(2):
            first = pl.multiple_of(quarter * (NCHAN // RADIX) + step * (4 * LANES) + 2 * pair * LANES, LANES)
            near, far = taps_ref[:, pl.ds(first, LANES)], taps_ref[:, pl.ds(first + LANES, LANES)]
            weights = [
                jnp.concatenate(
                    (
                        jnp.broadcast_to(near[tap : tap + 1], (4, LANES)),
                        jnp.broadcast_to(far[tap : tap + 1], (4, LANES)),
                    ),
                    axis=0,
                )
                for tap in range(TAPS)
            ]
            base = (index * 4 + pair * 2) * rows
            for start in range(0, count, BLOCK):
                lines = [wide[start + at, 8 * pair : 8 * pair + 8, :] for at in range(BLOCK + TAPS - 1)]
                for spectrum, value in enumerate(fir(lines, weights, BLOCK)):
                    filtered[pl.ds(base + start + spectrum, 8, stride=count), :] = value
        return carry

    fetch = pltpu.make_async_copy(table_ref.at[step], table, arrived)
    fetch.start()
    lax.fori_loop(0, 2 * RADIX, filter_lines, 0)

    def split_line(index, carry):
        line, start = index // (rows // CUT), pl.multiple_of(index % (rows // CUT) * CUT, CUT)

        def samples_of(part, quarter):
            first = pl.multiple_of(((part * RADIX + quarter) * 4 + line) * rows + start, CUT)
            return filtered[pl.ds(first, CUT), :]

        even, odd, twist = [], [], []
        for part in range(2):
            one, two, three, four = (samples_of(part, quarter) for quarter in range(RADIX))
            s, u = one + three, two + four
            even.append((s + u, s - u))
            odd.append(one - three)
            twist.append(two - four)
        lines = (
            (even[0][0], even[1][0]),
            (odd[0] + twist[1], odd[1] - twist[0]),
            (even[0][1], even[1][1]),
            (odd[0] - twist[1], odd[1] + twist[0]),
        )
        for rest in range(RADIX):
            for part in range(2):
                at = pl.ds(pl.multiple_of((4 * part + line) * LANES, LANES), LANES)
                high, low = halves(lines[rest][part])
                split[rest, pl.ds(start, CUT), at] = high
                split[rest, pl.ds(pl.multiple_of(rows + start, CUT), CUT), at] = low
        return carry

    lax.fori_loop(0, 4 * (rows // CUT), split_line, 0)

    @pl.when(step == 0)
    def _():
        total[...] = jnp.zeros_like(total)

    fetch.wait()

    def transform(rest, carry):
        total[rest] += jnp.dot(split[rest], table[rest], preferred_element_type=jnp.float32)
        return carry

    lax.fori_loop(0, RADIX, transform, 0)

    @pl.when(step == STEPS - 1)
    def _():
        lane = lax.broadcasted_iota(jnp.int32, (rows, LANES), 1)

        def summed(rest):
            both = total[rest, :rows, :] + total[rest, rows:, :]
            return both[:, :LANES] + both[:, LANES:]

        for parity in range(2):
            one, two = summed(parity), summed(parity + 2)
            real = jnp.where(lane < 64, one, two)
            imag = pltpu.roll(jnp.where(lane < 64, two, one), 64, 1)
            words = []
            for station in range(STATIONS_HERE):
                mask = good_ref[tile_ref[0], chan_ref[0] * STATIONS_HERE + station].astype(jnp.float32)
                at = slice(station * count, (station + 1) * count)
                words += [real[at] * mask, imag[at] * mask]
            words = jnp.concatenate(words, axis=0)
            for row in range(half):
                tile = words[row * LANES : (row + 1) * LANES].T
                for core in range(2):
                    for low_y in range(2):
                        slot = jnp.where(low_y_ref[0] == low_y, 0, 2 * half) + core * 4 * half
                        target = pl.ds(slot + parity * half + row, PEERS // 2, stride=8 * half)
                        start = (2 * core + low_y) * (PEERS // 2)
                        out_ref[target, :] = tile[start : start + PEERS // 2]


def channelise(first, count, place, good, samples, taps, table, earlier):
    out_rows = PEERS * 4 * (count // 16)
    return pl.pallas_call(
        functools.partial(channelise_kernel, count),
        grid=(STEPS,),
        in_specs=[
            pl.BlockSpec(memory_space=pltpu.SMEM),
            pl.BlockSpec(memory_space=pltpu.SMEM),
            pl.BlockSpec(memory_space=pltpu.SMEM),
            pl.BlockSpec(memory_space=pltpu.SMEM),
            pl.BlockSpec(
                (pl.Element(2), pl.Element(count + TAPS - 1), pl.Element(RADIX), pl.Element(16), pl.Element(LANES)),
                lambda q: (0, first, 0, 16 * q, 0),
            ),
            pl.BlockSpec((TAPS, NCHAN), lambda q: (0, 0)),
            pl.BlockSpec(memory_space=pl.ANY),
            pl.BlockSpec(memory_space=pl.ANY),
        ],
        out_specs=pl.BlockSpec((out_rows, LANES), lambda q: (0, 0)),
        out_shape=jax.ShapeDtypeStruct((out_rows, LANES), jnp.float32),
        scratch_shapes=[
            pltpu.VMEM((count + TAPS - 1, 16, LANES), jnp.float32),
            pltpu.VMEM((2 * RADIX * 16 * count, LANES), jnp.float32),
            pltpu.VMEM((RADIX, 2 * STATIONS_HERE * count, 8 * LANES), jnp.bfloat16),
            pltpu.VMEM((RADIX, 2 * STATIONS_HERE * count, 2 * LANES), jnp.float32),
            pltpu.VMEM((RADIX, 8 * LANES, 2 * LANES), jnp.bfloat16),
            pltpu.SemaphoreType.DMA,
        ],
        compiler_params=pltpu.CompilerParams(vmem_limit_bytes=VMEM),
        cost_estimate=pl.CostEstimate(
            flops=125_000_000 * count, bytes_accessed=7_000_000 + 60_000 * count, transcendentals=0
        ),
        name="channelise",
    )(good, *place, samples, taps, table, earlier)


def correlate_kernel(tile_ref, low_y_ref, *refs):
    pieces, (out_ref, stations, left, right) = (refs[:4], refs[4:8]), refs[8:]
    parity = pl.program_id(0)
    side, low_y = tile_ref[0], low_y_ref[0]
    lane = lax.broadcasted_iota(jnp.int32, (PEERS // 2, LANES), 1)
    column = lax.broadcasted_iota(jnp.int32, (256, LANES), 1)

    for which in range(4):
        slot = 2 * (side if which % 2 == 0 else 1 - side)
        base = 8 * (low_y if which < 2 else 1 - low_y)
        for part, (_, count) in enumerate(PARTS):
            half = count // 16
            buffer = stations.at[slot + part]
            for core in range(2):
                for station in range(STATIONS_HERE):
                    row = parity * half + station * half // STATIONS_HERE
                    word = pieces[part][which][pl.ds(core * 2 * half + row, PEERS // 2, stride=4 * half), :]
                    if part == 1:
                        word = word if station % 2 == 0 else pltpu.roll(word, 64, 1)
                        word = jnp.where(lane < 64, word, 0.0)
                    buffer[pl.ds(base + core * 4 + station, PEERS // 2, stride=16), :] = word

    mine = pl.ds(pl.multiple_of(side * 256, 256), 256)
    for which in range(2):
        for part in range(2):
            at = [slice((2 * term + part) * LANES, (2 * term + part + 1) * LANES) for term in range(3)]
            whole = stations[2 * which + part]
            high, low = halves(whole)
            block = slice(512 * which, 512 * which + 512)
            right[block, at[0]] = high
            right[block, at[1]] = high
            right[block, at[2]] = low
            value = stations[2 * which + part, mine, :]
            if part == 0:
                swapped = pltpu.roll(value, 64, 1)
                turned = jnp.where(column < 64, swapped, -swapped)
            else:
                turned = jnp.where(
                    column < 32, pltpu.roll(value, 96, 1), jnp.where(column < 64, -pltpu.roll(value, 32, 1), 0.0)
                )
            for start, operand in ((256 * which, value), (512 + 256 * which, turned)):
                high, low = halves(operand * (1.0 / SPECTRA))
                block = slice(start, start + 256)
                left[block, at[0]] = high
                left[block, at[1]] = low
                left[block, at[2]] = high

    def product(a, b):
        return lax.dot_general(a, b, (((1,), (1,)), ((), ())), preferred_element_type=jnp.float32)

    for at in range(0, 512, 256):
        both = [product(left[...], right[512 * q + at : 512 * q + at + 256, :]) for q in range(2)]
        real = [[both[q][256 * p : 256 * p + 256] for q in range(2)] for p in range(2)]
        imag = [[both[q][512 + 256 * p : 768 + 256 * p] for q in range(2)] for p in range(2)]
        planes = (
            real[0][0] + real[1][1],
            real[0][0] - real[1][1],
            real[0][1] + real[1][0],
            imag[0][1] - imag[1][0],
            imag[0][0] + imag[1][1],
            imag[0][0] - imag[1][1],
            imag[0][1] + imag[1][0],
            real[1][0] - real[0][1],
        )
        for index, plane in enumerate(planes):
            out_ref[0, index, :, at : at + 256] = plane.astype(jnp.bfloat16)


def correlate(tile, low_y, pieces):
    specs = [pl.BlockSpec((PEERS * count // 8, LANES), lambda c: (0, 0)) for _, count in PARTS for _ in range(4)]
    return pl.pallas_call(
        correlate_kernel,
        grid=(2,),
        in_specs=[pl.BlockSpec(memory_space=pltpu.SMEM)] * 2 + specs,
        out_specs=pl.BlockSpec((1, 8, 256, 512), lambda c: (c, 0, 0, 0)),
        out_shape=jax.ShapeDtypeStruct((2, 8, 256, 512), jnp.bfloat16),
        scratch_shapes=[
            pltpu.VMEM((4, 512, LANES), jnp.float32),
            pltpu.VMEM((1024, 6 * LANES), jnp.bfloat16),
            pltpu.VMEM((1024, 6 * LANES), jnp.bfloat16),
        ],
        compiler_params=pltpu.CompilerParams(vmem_limit_bytes=SMALL_VMEM),
        cost_estimate=pl.CostEstimate(flops=3_300_000_000, bytes_accessed=8_000_000, transcendentals=0),
        name="correlate",
    )(tile, low_y, *pieces)


def after(value, token):
    return pl.pallas_call(
        lambda value_ref, token_ref, out_ref: None,
        in_specs=[pl.BlockSpec(memory_space=pl.ANY), pl.BlockSpec(memory_space=pl.ANY)],
        out_specs=pl.BlockSpec(memory_space=pl.ANY),
        out_shape=jax.ShapeDtypeStruct(value.shape, value.dtype),
        input_output_aliases={0: 0},
        name="after",
    )(value, token)


def moves(sizes, target):
    pairs = []
    for z in range(sizes["z"]):
        for x in range(sizes["x"]):
            for y in range(4):
                for core in range(2):
                    source, goal = (
                        (((z * sizes["x"] + x) * 2 + at % 2) * 2 + core) * 2 + at // 2 for at in (y, target(y) % 4)
                    )
                    pairs.append((source, goal))
    return pairs


def on_device(sizes, voltages, filter_taps, input_good):
    table = jnp.asarray(transform_table())
    tile, low_y = lax.axis_index("yh"), lax.axis_index("yl")
    chan = lax.axis_index(("z", "x", "yl", "core"))
    samples = voltages.reshape(2, STATIONS_HERE, FRAMES, NCHAN // LANES, LANES)
    samples = samples.transpose(0, 2, 3, 1, 4).reshape(2, FRAMES, RADIX, LANES // RADIX, LANES)
    chan, tile, low_y = (index.reshape(1).astype(jnp.int32) for index in (chan, tile, low_y))
    swap = moves(sizes, lambda y: y + 2)
    pair = moves(sizes, lambda y: y ^ 1)
    cross = moves(sizes, lambda y: y - 1 if y % 2 == 0 else y + 1)
    pieces, earlier, token = [], filter_taps, None
    for first, count in PARTS:
        width = count // 8
        earlier = channelise(first, count, (chan, tile, low_y), input_good.T, samples, filter_taps, table, earlier)
        spectra = earlier if token is None else after(earlier, token)
        spectra = spectra.reshape(PEERS, 2 * width, LANES)
        joined = lax.all_to_all(spectra, GROUP, split_axis=0, concat_axis=0, tiled=True)
        token = joined[0, :8]
        near, far = (joined[:, at : at + width].reshape(-1, LANES) for at in (0, width))
        pieces += [near] + [lax.ppermute(block, AXES, pairs) for block, pairs in ((near, swap), (far, pair), (far, cross))]
    return correlate(tile, low_y, pieces)


def solution(mesh):
    sizes = {"z": 8, "x": 4, "yl": 2, "core": 2, "yh": 2}
    fine = Mesh(mesh.devices.reshape(tuple(sizes[axis] for axis in AXES)), AXES)
    in_specs = (P(None, ("z", "x", "yl", "core"), "yh", None), P(), P())
    out_specs = P(("z", "x", "yl", "core"), None, "yh", None)
    return jax.shard_map(
        functools.partial(on_device, sizes), mesh=fine, in_specs=in_specs, out_specs=out_specs, check_vma=False
    )
```
